32 devices in a mesh: dp: 4 (over y, x), expert: 8 (over z, core).
Axes of the slice: x: 2, y: 2, z: 4, core: 2. Of those that a mesh axis runs over, the one named last changes fastest.
Arguments:
- tokens: bfloat16 [2048, 1536], P(('dp', 'expert')), may hold values from -6 to 6
- expert_ids: int32 [2048, 2], P(('dp', 'expert')), may hold values from 0 to 7, all different within a row; in each aligned block of 64 rows (0 to 63, 64 to 127, ...) at most 17 rows name the same one
- gate_weights: float32 [2048, 2], P(('dp', 'expert')), may hold values from 0.2 to 1
- token_mass: float32 [2048], P(('dp', 'expert')), may hold values from 0.25 to 4
- out_cotangent: bfloat16 [2048, 1536], P(('dp', 'expert')), may hold values from -6 to 6
- placement: int32 [8], replicated, may hold values from 0 to 7, as said below
- w_in: bfloat16 [8, 1536, 6144], P('expert', None, 'dp'), may hold values from -0.15625 to 0.15625
- w_out: bfloat16 [8, 6144, 1536], P('expert', 'dp'), may hold values from -0.078125 to 0.078125
- m_in: bfloat16 [8, 1536, 6144], P('expert', None, 'dp'), may hold values from -6 to 6
- v_in: bfloat16 [8, 1536, 6144], P('expert', None, 'dp'), may hold values from 0.5 to 4
- m_out: bfloat16 [8, 6144, 1536], P('expert', 'dp'), may hold values from -6 to 6
- v_out: bfloat16 [8, 6144, 1536], P('expert', 'dp'), may hold values from 0.5 to 4
Outputs:
- expert_output: bfloat16 [2048, 1536], P(('dp', 'expert'))
- token_grad: bfloat16 [2048, 1536], P(('dp', 'expert'))
- m_in_new: bfloat16 [8, 1536, 6144], P('expert', None, 'dp')
- v_in_new: bfloat16 [8, 1536, 6144], P('expert', None, 'dp')
- m_out_new: bfloat16 [8, 6144, 1536], P('expert', 'dp')
- v_out_new: bfloat16 [8, 6144, 1536], P('expert', 'dp')
The draws below stay inside these ranges and needn't reach their ends.
Inputs may be any that keep to these rules, and one draw needn't show every extreme that they name: `expert_ids`: within the rows of one device no expert is named by more than 17 ids, and the two ids of a token differ. placement is its own inverse: slot s holds expert s or expert s + 8 / 2 (for s < 4; symmetrically above), and both kinds of slot occur.
All inputs are finite; a program needn't handle non-finite values.
Results may differ from the reference program's by a relative error of at most 0.015.
Values may be sent and summed in bfloat16 or wider, within the bound.
A program may use at most 128 MiB of HBM per device.

```python
import math
import jax
import jax.numpy as jnp
import numpy as np
from jax import lax

D = 1536
FF = 6144
EXPERTS = 8
TOK_DEV = 64
CAP = 17
ROWS = 544
TOKENS = 2048
N_DP = 4
N_EXPERT = 8


def draw_placement(key, part):
    half_count = EXPERTS // 2
    swap_flags = jax.random.randint(key, (half_count,), 0, 2, dtype=jnp.int32)
    first_pair = jax.random.randint(jax.random.fold_in(key, 7), (), 0, half_count, dtype=jnp.int32)
    pair_index = jnp.arange(half_count, dtype=jnp.int32)
    swap_flags = jnp.where(pair_index == first_pair, 1, jnp.where(pair_index == (first_pair + 1) % half_count, 0, swap_flags))
    low_slots = pair_index + swap_flags * half_count
    high_slots = pair_index + half_count - swap_flags * half_count
    return jnp.concatenate([low_slots, high_slots]).astype(jnp.int32)


def block_scale(key, extent, split, low, top_value):
    def one(axis_at, blocks):
        draws = jax.random.uniform(jax.random.fold_in(jax.random.fold_in(key, 6), axis_at), (blocks,), jnp.float32, low / len(split), top_value / len(split))
        return jnp.repeat(jnp.exp(draws), extent[axis_at] // blocks).reshape((-1,) + (1,) * (len(extent) - axis_at - 1))

    factor_of = one(*split[0])
    for cut in split[1:]:
        factor_of = factor_of * one(*cut)
    return factor_of


def routed_block(rng, own, number, rows, count, top, most, lean):
    order = jax.random.permutation(rng, count)
    heavy_load, usual = load_shares(count, rows * top, most, lean, True), load_shares(count, rows * top, most, lean, False)
    places = jnp.arange(count)

    def named(lengths, rotation):
        used = int((lengths > 0).sum())
        fixed = max(1, used // 4)
        shifted = fixed + (places - fixed + rotation * (used - fixed)) % max(1, count - fixed)
        return jnp.zeros((count,), jnp.int32).at[order[jnp.where(places < fixed, places, shifted)]].set(jnp.asarray(lengths, jnp.int32))

    lengths = jnp.where(number % 4 == 0, named(heavy_load, number // 4), named(usual, number - number // 4 - 1))
    mixed = jax.random.permutation(jax.random.fold_in(own, 3), count)
    source_of, receiver = mixed[0:count // 2 * 2:2], mixed[1:count // 2 * 2:2]
    margin = jnp.minimum(lengths[source_of] - 1, most - lengths[receiver]) // 2
    margin = jnp.where((source_of == order[0]) | (receiver == order[0]) | (lengths[receiver] == 0), 0, jnp.maximum(margin, 0))
    shifted = jax.random.randint(jax.random.fold_in(own, 4), (count // 2,), 0, 1 << 20) % (margin + 1)
    lengths = lengths.at[source_of].add(-shifted).at[receiver].add(shifted)
    items = jnp.searchsorted(jnp.cumsum(lengths), jnp.arange(rows * top), side="right").astype(jnp.int32)
    grid = items.reshape(top, rows).T
    grid = grid[jax.random.permutation(jax.random.fold_in(own, 1), rows)]
    rotation = jax.random.randint(jax.random.fold_in(own, 2), (rows, 1), 0, top)
    return jnp.take_along_axis(grid, (jnp.arange(top)[None, :] + rotation) % top, axis=1)


def load_shares(count, total, reach, lean, full):
    weights = [(1 << 20) // math.isqrt(grade ** lean) + 1 for grade in range(1, count + 1)]
    largest = reach if full else min(reach, max(-(-total // count), total * weights[0] // sum(weights)))
    least = 1 if total - largest >= count - 1 else 0
    counts, spare = [largest] + [least] * (count - 1), total - largest - least * (count - 1)
    while spare > 0:
        movable = [i for i in range(1, count) if counts[i] < largest] or [i for i in range(1, count) if counts[i] < reach]
        pool, left = sum([weights[i] for i in movable]), spare
        for i in movable:
            extra = min(reach - counts[i], max(1, left * weights[i] // pool), spare)
            counts[i] = counts[i] + extra
            spare = spare - extra
    return np.array(counts)


def gaussian(own_key, shape, deviation, bound, cuts=(), kind=jnp.bfloat16):
    values = deviation * jax.random.normal(own_key, shape, jnp.float32)
    if cuts:
        values = values * block_scale(own_key, shape, cuts, -0.22, 0.18)
    return jnp.clip(values, -bound, bound).astype(kind)


def setup_inputs(seed: int = 0) -> dict:
    key_list = jax.random.split(jax.random.key(seed), 13)
    tokens = gaussian(key_list[0], (TOKENS, D), 1.0, 6.0, ((0, 32),))
    expert_ids_keys = jax.random.split(jax.random.fold_in(key_list[1], 1), TOKENS // TOK_DEV)
    expert_ids_turns = jax.random.permutation(jax.random.fold_in(key_list[1], 3), TOKENS // TOK_DEV)
    expert_ids = jax.vmap(lambda own, number: routed_block(jax.random.fold_in(key_list[1], 2), own, number, TOK_DEV, EXPERTS, 2, CAP, 2))(expert_ids_keys, expert_ids_turns).reshape((TOKENS, 2))
    gate_weights = jnp.clip(0.2 + 0.8 * jax.random.uniform(key_list[2], (TOKENS, 2), jnp.float32) ** block_scale(key_list[2], (TOKENS, 2), ((0, 32),), -0.2, 0.2), 0.2, 1.0)
    token_mass = jnp.clip(jnp.exp(math.log(4.0) - 2.7725887 * jax.random.uniform(key_list[3], (TOKENS,), jnp.float32) ** block_scale(key_list[3], (TOKENS,), ((0, 32),), -0.2, 0.2)), 0.25, 4.0)
    out_cotangent = gaussian(key_list[4], (TOKENS, D), 1.0, 6.0, ((0, 32),))
    placement = draw_placement(jax.random.fold_in(key_list[12], 71), 0)
    w_in = gaussian(key_list[6], (EXPERTS, D, FF), D ** -0.5, 0.15625, ((0, 8), (2, 4)))
    w_out = gaussian(key_list[7], (EXPERTS, FF, D), FF ** -0.5, 0.078125, ((0, 8), (1, 4)))
    m_in = gaussian(key_list[8], (EXPERTS, D, FF), 1.0, 6.0, ((0, 8), (2, 4)))
    v_in = jnp.clip(jnp.exp(math.log(4.0) - 2.0794415 * jax.random.uniform(key_list[9], (EXPERTS, D, FF), jnp.float32) ** block_scale(key_list[9], (EXPERTS, D, FF), ((0, 8), (2, 4)), -0.2, 0.2)), 0.5, 4.0).astype(jnp.bfloat16)
    m_out = gaussian(key_list[10], (EXPERTS, FF, D), 1.0, 6.0, ((0, 8), (1, 4)))
    v_out = jnp.clip(jnp.exp(math.log(4.0) - 2.0794415 * jax.random.uniform(key_list[11], (EXPERTS, FF, D), jnp.float32) ** block_scale(key_list[11], (EXPERTS, FF, D), ((0, 8), (1, 4)), -0.2, 0.2)), 0.5, 4.0).astype(jnp.bfloat16)
    return {"tokens": tokens, "expert_ids": expert_ids, "gate_weights": gate_weights, "token_mass": token_mass, "out_cotangent": out_cotangent, "placement": placement, "w_in": w_in, "w_out": w_out, "m_in": m_in, "v_in": v_in, "m_out": m_out, "v_out": v_out}


def gelu_tanh(values):
    return jax.nn.gelu(values, approximate=True)

def reference(tokens, expert_ids, gate_weights, token_mass, out_cotangent, placement, w_in, w_out, m_in, v_in, m_out, v_out):
    n_dev = N_DP * N_EXPERT
    model_width = tokens.shape[1]
    flat_expert = expert_ids.reshape(-1).astype(jnp.int32)
    onehot = (flat_expert[:, None] == jnp.arange(EXPERTS, dtype=jnp.int32)[None, :]).astype(jnp.int32)
    per_device = onehot.reshape(n_dev, 2 * TOK_DEV, EXPERTS)
    earlier = jnp.cumsum(per_device, axis=1) - per_device
    rank_in = lax.optimization_barrier(jnp.sum(earlier * per_device, axis=2)).reshape(-1).astype(jnp.int32)
    source = (jnp.arange(2 * TOKENS, dtype=jnp.int32) // (2 * TOK_DEV)).astype(jnp.int32)
    row_index = (source * CAP + rank_in).astype(jnp.int32)
    entries = jnp.repeat(tokens, 2, axis=0)
    scaled = (gate_weights * token_mass[:, None])[:, :, None] * out_cotangent[:, None, :].astype(jnp.float32)
    cot_rows = scaled.reshape(2 * TOKENS, model_width).astype(jnp.bfloat16)
    buf_x = jnp.zeros((EXPERTS, ROWS, model_width), jnp.bfloat16).at[flat_expert, row_index].set(entries)
    buf_g = jnp.zeros((EXPERTS, ROWS, model_width), jnp.bfloat16).at[flat_expert, row_index].set(cot_rows)
    shard_width = FF // N_DP

    def split_sum(left, right):
        total = jnp.zeros((left.shape[0], right.shape[1]), jnp.float32)
        for j in range(N_DP):
            partial_value = jnp.dot(left[:, j * shard_width:(j + 1) * shard_width], right[j * shard_width:(j + 1) * shard_width], preferred_element_type=jnp.float32).astype(jnp.bfloat16)
            total = total + lax.optimization_barrier(partial_value).astype(jnp.float32)
        return total.astype(jnp.bfloat16)

    def one_expert(items):
        rows_x, rows_g, weight_in, weight_out, mom_in, sec_in, mom_out, sec_out = items
        hidden = jnp.dot(rows_x, weight_in, preferred_element_type=jnp.float32)
        active = gelu_tanh(hidden).astype(jnp.bfloat16)
        out_rows = split_sum(active, weight_out)
        grad_act = jnp.dot(rows_g, weight_out.T, preferred_element_type=jnp.float32)
        _, pullback = jax.vjp(gelu_tanh, hidden)
        grad_hidden = pullback(grad_act)[0].astype(jnp.bfloat16)
        in_rows = split_sum(grad_hidden, weight_in.T)
        grad_in = jnp.dot(rows_x.T, grad_hidden, preferred_element_type=jnp.float32)
        grad_out = jnp.dot(active.T, rows_g, preferred_element_type=jnp.float32)
        new_mi = (0.9 * mom_in.astype(jnp.float32) + 0.1 * grad_in).astype(jnp.bfloat16)
        new_vi = (0.999 * sec_in.astype(jnp.float32) + 0.001 * grad_in * grad_in).astype(jnp.bfloat16)
        new_mo = (0.9 * mom_out.astype(jnp.float32) + 0.1 * grad_out).astype(jnp.bfloat16)
        new_vo = (0.999 * sec_out.astype(jnp.float32) + 0.001 * grad_out * grad_out).astype(jnp.bfloat16)
        return (out_rows, in_rows, new_mi, new_vi, new_mo, new_vo)
    out_all, in_all, mi_new, vi_new, mo_new, vo_new = lax.map(one_expert, (buf_x, buf_g, w_in, w_out, m_in, v_in, m_out, v_out))
    picks_y = out_all[flat_expert, row_index].astype(jnp.float32).reshape(TOKENS, 2, model_width)
    expert_output = lax.optimization_barrier(jnp.sum(picks_y * gate_weights[:, :, None], axis=1)).astype(jnp.bfloat16)
    picks_x = in_all[flat_expert, row_index].astype(jnp.float32).reshape(TOKENS, 2, model_width)
    token_grad = lax.optimization_barrier(jnp.sum(picks_x, axis=1)).astype(jnp.bfloat16)
    slot_order = placement.astype(jnp.int32)
    return (expert_output, token_grad, mi_new[slot_order], vi_new[slot_order], mo_new[slot_order], vo_new[slot_order])
```

```python
import functools

import jax
import jax.numpy as jnp
from jax import lax
from jax.sharding import PartitionSpec as P

GROUP = 4


def gelu_tanh(values):
    return jax.nn.gelu(values, approximate=True)


def gelu_backward(hidden, grad_act):
    _, pullback = jax.vjp(gelu_tanh, hidden)
    return pullback(grad_act)[0].astype(jnp.bfloat16)


def contract_first(left, right):
    return lax.dot_general(
        left, right, (((0,), (0,)), ((), ())), preferred_element_type=jnp.float32
    )


def contract_last(left, right):
    return lax.dot_general(
        left, right, (((1,), (1,)), ((), ())), preferred_element_type=jnp.float32
    )


def route_of(pattern, pairs, count):
    half = count // 2
    dest = list(range(count))
    for bit, low in enumerate(pairs):
        if pattern >> bit & 1:
            dest[low], dest[low + half] = low + half, low
    return [(src, dst) for src, dst in enumerate(dest)]


def exchange(arrays, pattern, pairs, count):
    if pattern == 0:
        return tuple(arrays)
    route = route_of(pattern, pairs, count)
    return tuple(lax.ppermute(a, "expert", route) for a in arrays)


def tail(pattern, pairs, args):
    rows_x, rows_g, active, grad_hidden, select, gate_weights, w_in, w_out = args[:8]
    m_in, v_in, m_out, v_out = args[8:]
    count = lax.axis_size("expert")
    width = rows_x.shape[1]
    tok_count = gate_weights.shape[0]
    capacity = select.shape[0] // count
    grad_out = contract_first(active, rows_g)
    new_mo = (0.9 * m_out[0].astype(jnp.float32) + 0.1 * grad_out).astype(jnp.bfloat16)[None]
    new_vo = (0.999 * v_out[0].astype(jnp.float32) + 0.001 * grad_out * grad_out).astype(
        jnp.bfloat16
    )[None]
    grad_in = contract_first(rows_x, grad_hidden)
    new_mi = (0.9 * m_in[0].astype(jnp.float32) + 0.1 * grad_in).astype(jnp.bfloat16)[None]
    new_vi = (0.999 * v_in[0].astype(jnp.float32) + 0.001 * grad_in * grad_in).astype(
        jnp.bfloat16
    )[None]
    moments = exchange((new_mi, new_vi, new_mo, new_vo), pattern, pairs, count)

    def home(partial):
        mine = lax.psum_scatter(partial.astype(jnp.bfloat16), "dp", scatter_dimension=0, tiled=True)
        back = lax.all_to_all(
            mine.reshape(count, capacity, width), "expert", split_axis=0, concat_axis=0, tiled=True
        )
        picks = contract_first(select, back.reshape(count * capacity, width))
        return picks.reshape(tok_count, 2, width)

    picks_y = home(jnp.dot(active, w_out[0], preferred_element_type=jnp.float32))
    picks_x = home(contract_last(grad_hidden, w_in[0]))
    expert_output = jnp.sum(picks_y * gate_weights[:, :, None], axis=1).astype(jnp.bfloat16)
    token_grad = jnp.sum(picks_x, axis=1).astype(jnp.bfloat16)
    return (expert_output, token_grad) + moments


def on_device(
    tokens,
    expert_ids,
    gate_weights,
    token_mass,
    out_cotangent,
    placement,
    w_in,
    w_out,
    m_in,
    v_in,
    m_out,
    v_out,
):
    tok_count, model_width = tokens.shape
    count = lax.axis_size("expert")
    half = count // 2
    capacity = 2 * tok_count // count + 1
    block_rows = count * capacity

    flat = expert_ids.reshape(-1)
    n_entries = flat.shape[0]
    order = jnp.arange(n_entries, dtype=jnp.int32)
    earlier = (flat[:, None] == flat[None, :]) & (order[None, :] < order[:, None])
    rank_in = jnp.sum(earlier.astype(jnp.int32), axis=1)
    row_index = flat * capacity + rank_in
    hit = row_index[None, :] == jnp.arange(block_rows, dtype=jnp.int32)[:, None]
    select = hit.astype(jnp.bfloat16)
    scale = jnp.sum(
        jnp.where(hit, (gate_weights * token_mass[:, None]).reshape(1, -1), 0.0), axis=1
    )
    by_token = jnp.sum(select.reshape(block_rows, tok_count, 2), axis=2)
    send_x = jnp.dot(by_token, tokens, preferred_element_type=jnp.float32).astype(jnp.bfloat16)
    cot = jnp.dot(by_token, out_cotangent, preferred_element_type=jnp.float32)
    send_g = (scale[:, None] * cot).astype(jnp.bfloat16)
    send = jnp.concatenate([send_x, send_g], axis=1).reshape(count, capacity, 2 * model_width)
    recv = lax.all_to_all(send, "expert", split_axis=0, concat_axis=0, tiled=True)
    rows = lax.all_gather(recv.reshape(block_rows, 2 * model_width), "dp", axis=0, tiled=True)
    rows_x, rows_g = rows[:, :model_width], rows[:, model_width:]

    hidden = jnp.dot(rows_x, w_in[0], preferred_element_type=jnp.float32)
    active = gelu_tanh(hidden).astype(jnp.bfloat16)
    grad_hidden = gelu_backward(hidden, contract_last(rows_g, w_out[0]))

    swapped = (placement[:half] != jnp.arange(half, dtype=jnp.int32)).astype(jnp.int32)
    args = (rows_x, rows_g, active, grad_hidden, select, gate_weights, w_in, w_out)
    args += (m_in, v_in, m_out, v_out)
    results = None
    for start in range(0, half, GROUP):
        pairs = tuple(range(start, min(start + GROUP, half)))
        index = jnp.sum(swapped[start : start + len(pairs)] << jnp.arange(len(pairs)))
        patterns = list(range(1 << len(pairs)))
        if len(pairs) == half:
            patterns, index = patterns[1:-1], index - 1
        if results is None:
            branches = [functools.partial(tail, p, pairs) for p in patterns]
            results = lax.switch(index, branches, args)
        else:
            branches = [
                lambda a, p=p, pairs=pairs: exchange(a, p, pairs, count)
                for p in patterns
            ]
            results = results[:2] + tuple(lax.switch(index, branches, results[2:]))
    return tuple(results)


def solution(mesh):
    return jax.shard_map(
        on_device,
        mesh=mesh,
        in_specs=(
            P(("dp", "expert"), None),
            P(("dp", "expert"), None),
            P(("dp", "expert"), None),
            P(("dp", "expert")),
            P(("dp", "expert"), None),
            P(),
            P("expert", None, "dp"),
            P("expert", "dp", None),
            P("expert", None, "dp"),
            P("expert", None, "dp"),
            P("expert", "dp", None),
            P("expert", "dp", None),
        ),
        out_specs=(
            P(("dp", "expert"), None),
            P(("dp", "expert"), None),
            P("expert", None, "dp"),
            P("expert", None, "dp"),
            P("expert", "dp", None),
            P("expert", "dp", None),
        ),
        check_vma=False,
    )
```

```python
import functools

import jax
import jax.numpy as jnp
from jax import lax
from jax.sharding import PartitionSpec as P

GROUP = 4


def gelu_tanh(values):
    return jax.nn.gelu(values, approximate=True)


def gelu_backward(hidden, grad_act):
    _, pullback = jax.vjp(gelu_tanh, hidden)
    return pullback(grad_act)[0].astype(jnp.bfloat16)


def contract_first(left, right):
    return lax.dot_general(
        left, right, (((0,), (0,)), ((), ())), preferred_element_type=jnp.float32
    )


def contract_last(left, right):
    return lax.dot_general(
        left, right, (((1,), (1,)), ((), ())), preferred_element_type=jnp.float32
    )


def exchange(arrays, pattern, pairs, count, moves):
    half = count // 2
    route = []
    for bit, low in enumerate(pairs):
        if pattern >> bit & 1:
            route += [(low, low + half), (low + half, low)]
    if not route:
        return tuple(arrays)
    return tuple(jnp.where(moves, lax.ppermute(a, "expert", route), a) for a in arrays)


def tail(pattern, pairs, args):
    rows_x, active, grad_hidden, select, gate_weights, moves, w_in, w_out = args[:8]
    m_in, v_in, new_mo, new_vo = args[8:]
    count = lax.axis_size("expert")
    width = rows_x.shape[1]
    tok_count = gate_weights.shape[0]
    capacity = select.shape[0] // count
    moved_out = exchange((new_mo, new_vo), pattern, pairs, count, moves)
    grad_in = contract_first(rows_x, grad_hidden)
    new_mi = (0.9 * m_in[0].astype(jnp.float32) + 0.1 * grad_in).astype(jnp.bfloat16)[None]
    new_vi = (0.999 * v_in[0].astype(jnp.float32) + 0.001 * grad_in * grad_in).astype(
        jnp.bfloat16
    )[None]
    moved_in = exchange((new_mi, new_vi), pattern, pairs, count, moves)

    partial_y = jnp.dot(active, w_out[0], preferred_element_type=jnp.float32)
    partial_z = contract_last(grad_hidden, w_in[0])
    both = jnp.concatenate(
        [partial_y.astype(jnp.bfloat16), partial_z.astype(jnp.bfloat16)], axis=1
    )
    mine = lax.psum_scatter(both, "dp", scatter_dimension=0, tiled=True)
    back = lax.all_to_all(
        mine.reshape(count, capacity, 2 * width), "expert", split_axis=0, concat_axis=0, tiled=True
    )
    picks = contract_first(select, back.reshape(count * capacity, 2 * width))
    picks = picks.reshape(tok_count, 2, 2 * width)
    expert_output = jnp.sum(picks[:, :, :width] * gate_weights[:, :, None], axis=1)
    token_grad = jnp.sum(picks[:, :, width:], axis=1)
    return (
        expert_output.astype(jnp.bfloat16),
        token_grad.astype(jnp.bfloat16),
    ) + moved_in + moved_out


def on_device(
    tokens,
    expert_ids,
    gate_weights,
    token_mass,
    out_cotangent,
    placement,
    w_in,
    w_out,
    m_in,
    v_in,
    m_out,
    v_out,
):
    tok_count, model_width = tokens.shape
    count = lax.axis_size("expert")
    half = count // 2
    capacity = 2 * tok_count // count + 1
    block_rows = count * capacity

    flat = expert_ids.reshape(-1)
    n_entries = flat.shape[0]
    order = jnp.arange(n_entries, dtype=jnp.int32)
    earlier = (flat[:, None] == flat[None, :]) & (order[None, :] < order[:, None])
    rank_in = jnp.sum(earlier.astype(jnp.int32), axis=1)
    row_index = flat * capacity + rank_in
    hit = row_index[None, :] == jnp.arange(block_rows, dtype=jnp.int32)[:, None]
    select = hit.astype(jnp.bfloat16)
    scale = jnp.sum(
        jnp.where(hit, (gate_weights * token_mass[:, None]).reshape(1, -1), 0.0), axis=1
    )
    by_token = jnp.sum(select.reshape(block_rows, tok_count, 2), axis=2)
    send_x = jnp.dot(by_token, tokens, preferred_element_type=jnp.float32).astype(jnp.bfloat16)
    cot = jnp.dot(by_token, out_cotangent, preferred_element_type=jnp.float32)
    send_g = (scale[:, None] * cot).astype(jnp.bfloat16)
    send = jnp.concatenate([send_x, send_g], axis=1).reshape(count, capacity, 2 * model_width)
    recv = lax.all_to_all(send, "expert", split_axis=0, concat_axis=0, tiled=True)
    rows = lax.all_gather(recv.reshape(block_rows, 2 * model_width), "dp", axis=0, tiled=True)
    rows_x, rows_g = rows[:, :model_width], rows[:, model_width:]

    hidden = jnp.dot(rows_x, w_in[0], preferred_element_type=jnp.float32)
    active = gelu_tanh(hidden).astype(jnp.bfloat16)
    grad_out = contract_first(active, rows_g)
    new_mo = (0.9 * m_out[0].astype(jnp.float32) + 0.1 * grad_out).astype(jnp.bfloat16)[None]
    new_vo = (0.999 * v_out[0].astype(jnp.float32) + 0.001 * grad_out * grad_out).astype(
        jnp.bfloat16
    )[None]

    grad_hidden = gelu_backward(hidden, contract_last(rows_g, w_out[0]))

    swapped = (placement[:half] != jnp.arange(half, dtype=jnp.int32)).astype(jnp.int32)
    my_slot = lax.axis_index("expert")
    moves = placement[my_slot] != my_slot
    args = (rows_x, active, grad_hidden, select, gate_weights)
    args += (moves & (my_slot % half < GROUP), w_in, w_out, m_in, v_in, new_mo, new_vo)
    results = None
    for start in range(0, half, GROUP):
        pairs = tuple(range(start, min(start + GROUP, half)))
        index = jnp.sum(swapped[start : start + len(pairs)] << jnp.arange(len(pairs)))
        patterns = list(range(1 << len(pairs)))
        if len(pairs) == half:
            patterns, index = patterns[1:-1], index - 1
        if results is None:
            branches = [functools.partial(tail, p, pairs) for p in patterns]
            results = lax.switch(index, branches, args)
        else:
            mine = (my_slot % half >= start) & (my_slot % half < start + len(pairs))
            branches = [
                lambda a, p=p, pairs=pairs: exchange(a[1:], p, pairs, count, a[0])
                for p in patterns
            ]
            results = results[:2] + tuple(lax.switch(index, branches, (moves & mine,) + results[2:]))
    return tuple(results)


def solution(mesh):
    return jax.shard_map(
        on_device,
        mesh=mesh,
        in_specs=(
            P(("dp", "expert"), None),
            P(("dp", "expert"), None),
            P(("dp", "expert"), None),
            P(("dp", "expert")),
            P(("dp", "expert"), None),
            P(),
            P("expert", None, "dp"),
            P("expert", "dp", None),
            P("expert", None, "dp"),
            P("expert", None, "dp"),
            P("expert", "dp", None),
            P("expert", "dp", None),
        ),
        out_specs=(
            P(("dp", "expert"), None),
            P(("dp", "expert"), None),
            P("expert", None, "dp"),
            P("expert", None, "dp"),
            P("expert", "dp", None),
            P("expert", "dp", None),
        ),
        check_vma=False,
    )
```

```python
import functools

import jax
import jax.numpy as jnp
from jax import lax
from jax.sharding import PartitionSpec as P

GROUP = 4


def gelu_tanh(values):
    return jax.nn.gelu(values, approximate=True)


def gelu_backward(hidden, grad_act):
    _, pullback = jax.vjp(gelu_tanh, hidden)
    return pullback(grad_act)[0].astype(jnp.bfloat16)


def contract_first(left, right):
    return lax.dot_general(
        left, right, (((0,), (0,)), ((), ())), preferred_element_type=jnp.float32
    )


def contract_last(left, right):
    return lax.dot_general(
        left, right, (((1,), (1,)), ((), ())), preferred_element_type=jnp.float32
    )


def exchange(arrays, pattern, pairs, count, moves):
    half = count // 2
    route = []
    for bit, low in enumerate(pairs):
        if pattern >> bit & 1:
            route += [(low, low + half), (low + half, low)]
    if not route:
        return tuple(arrays)
    return tuple(jnp.where(moves, lax.ppermute(a, "expert", route), a) for a in arrays)


def tail(pattern, pairs, args):
    rows_x, active, grad_hidden, select, gate_weights, moves, w_in, w_out = args[:8]
    m_in, v_in, new_mo, new_vo = args[8:]
    count = lax.axis_size("expert")
    width = rows_x.shape[1]
    tok_count = gate_weights.shape[0]
    capacity = select.shape[0] // count
    moved_out = exchange((new_mo, new_vo), pattern, pairs, count, moves)
    grad_in = contract_first(rows_x, grad_hidden)
    new_mi = (0.9 * m_in[0].astype(jnp.float32) + 0.1 * grad_in).astype(jnp.bfloat16)[None]
    new_vi = (0.999 * v_in[0].astype(jnp.float32) + 0.001 * grad_in * grad_in).astype(
        jnp.bfloat16
    )[None]
    moved_in = exchange((new_mi, new_vi), pattern, pairs, count, moves)

    partial_y = jnp.dot(active, w_out[0], preferred_element_type=jnp.float32)
    partial_z = contract_last(grad_hidden, w_in[0])
    both = jnp.concatenate(
        [partial_y.astype(jnp.bfloat16), partial_z.astype(jnp.bfloat16)], axis=1
    )
    shares = lax.all_to_all(
        both.reshape(lax.axis_size("dp"), count * capacity, 2 * width),
        "dp",
        split_axis=0,
        concat_axis=0,
        tiled=True,
    )
    mine = jnp.sum(shares.astype(jnp.float32), axis=0).astype(jnp.bfloat16)
    back = lax.all_to_all(
        mine.reshape(count, capacity, 2 * width), "expert", split_axis=0, concat_axis=0, tiled=True
    )
    picks = contract_first(select, back.reshape(count * capacity, 2 * width))
    picks = picks.reshape(tok_count, 2, 2 * width)
    expert_output = jnp.sum(picks[:, :, :width] * gate_weights[:, :, None], axis=1)
    token_grad = jnp.sum(picks[:, :, width:], axis=1)
    return (
        expert_output.astype(jnp.bfloat16),
        token_grad.astype(jnp.bfloat16),
    ) + moved_in + moved_out


def on_device(
    tokens,
    expert_ids,
    gate_weights,
    token_mass,
    out_cotangent,
    placement,
    w_in,
    w_out,
    m_in,
    v_in,
    m_out,
    v_out,
):
    tok_count, model_width = tokens.shape
    count = lax.axis_size("expert")
    half = count // 2
    capacity = 2 * tok_count // count + 1
    block_rows = count * capacity

    flat = expert_ids.reshape(-1)
    n_entries = flat.shape[0]
    order = jnp.arange(n_entries, dtype=jnp.int32)
    earlier = (flat[:, None] == flat[None, :]) & (order[None, :] < order[:, None])
    rank_in = jnp.sum(earlier.astype(jnp.int32), axis=1)
    row_index = flat * capacity + rank_in
    hit = row_index[None, :] == jnp.arange(block_rows, dtype=jnp.int32)[:, None]
    select = hit.astype(jnp.bfloat16)
    scale = jnp.sum(
        jnp.where(hit, (gate_weights * token_mass[:, None]).reshape(1, -1), 0.0), axis=1
    )
    by_token = jnp.sum(select.reshape(block_rows, tok_count, 2), axis=2)
    send_x = jnp.dot(by_token, tokens, preferred_element_type=jnp.float32).astype(jnp.bfloat16)
    cot = jnp.dot(by_token, out_cotangent, preferred_element_type=jnp.float32)
    send_g = (scale[:, None] * cot).astype(jnp.bfloat16)

    def dispatch(send):
        recv = lax.all_to_all(
            send.reshape(count, capacity, model_width),
            "expert",
            split_axis=0,
            concat_axis=0,
            tiled=True,
        )
        return lax.all_gather(recv.reshape(block_rows, model_width), "dp", axis=0, tiled=True)

    rows_x = dispatch(send_x)
    rows_g = dispatch(send_g)
    hidden = jnp.dot(rows_x, w_in[0], preferred_element_type=jnp.float32)
    active = gelu_tanh(hidden).astype(jnp.bfloat16)
    grad_out = contract_first(active, rows_g)
    new_mo = (0.9 * m_out[0].astype(jnp.float32) + 0.1 * grad_out).astype(jnp.bfloat16)[None]
    new_vo = (0.999 * v_out[0].astype(jnp.float32) + 0.001 * grad_out * grad_out).astype(
        jnp.bfloat16
    )[None]

    grad_hidden = gelu_backward(hidden, contract_last(rows_g, w_out[0]))

    swapped = (placement[:half] != jnp.arange(half, dtype=jnp.int32)).astype(jnp.int32)
    my_slot = lax.axis_index("expert")
    moves = placement[my_slot] != my_slot
    args = (rows_x, active, grad_hidden, select, gate_weights)
    args += (moves & (my_slot % half < GROUP), w_in, w_out, m_in, v_in, new_mo, new_vo)
    results = None
    for start in range(0, half, GROUP):
        pairs = tuple(range(start, min(start + GROUP, half)))
        index = jnp.sum(swapped[start : start + len(pairs)] << jnp.arange(len(pairs)))
        patterns = list(range(1 << len(pairs)))
        if len(pairs) == half:
            patterns, index = patterns[1:-1], index - 1
        if results is None:
            branches = [functools.partial(tail, p, pairs) for p in patterns]
            results = lax.switch(index, branches, args)
        else:
            mine = (my_slot % half >= start) & (my_slot % half < start + len(pairs))
            branches = [
                lambda a, p=p, pairs=pairs: exchange(a[1:], p, pairs, count, a[0])
                for p in patterns
            ]
            results = results[:2] + tuple(lax.switch(index, branches, (moves & mine,) + results[2:]))
    return tuple(results)


def solution(mesh):
    return jax.shard_map(
        on_device,
        mesh=mesh,
        in_specs=(
            P(("dp", "expert"), None),
            P(("dp", "expert"), None),
            P(("dp", "expert"), None),
            P(("dp", "expert")),
            P(("dp", "expert"), None),
            P(),
            P("expert", None, "dp"),
            P("expert", "dp", None),
            P("expert", None, "dp"),
            P("expert", None, "dp"),
            P("expert", "dp", None),
            P("expert", "dp", None),
        ),
        out_specs=(
            P(("dp", "expert"), None),
            P(("dp", "expert"), None),
            P("expert", None, "dp"),
            P("expert", None, "dp"),
            P("expert", "dp", None),
            P("expert", "dp", None),
        ),
        check_vma=False,
    )
```
